32 devices in a mesh: ctx: 16 (over z, y, core), head: 2 (over x).
Axes of the slice: x: 2, y: 2, z: 4, core: 2. Of those that a mesh axis runs over, the one named last changes fastest.
Arguments:
- queries: bfloat16 [2048, 4096], P(('ctx', 'head')), may hold values from -4.6 to 4.6
- key_states: bfloat16 [2048, 4096], P(('ctx', 'head')), may hold values from -4.6 to 4.6
- value_states: bfloat16 [2048, 4096], P(('ctx', 'head')), may hold values from -6 to 6
- out_grad: bfloat16 [2048, 4096], P(('ctx', 'head')), may hold values from -6 to 6
- random_blocks: int32 [64, 3], replicated, may hold values from 0 to 63, as said below
- global_blocks: int32 [4], replicated, may hold values from 0 to 63, as said below
Outputs:
- query_grad: bfloat16 [2048, 4096], P('ctx', 'head')
- key_grad: bfloat16 [2048, 4096], P('ctx', 'head')
- value_grad: bfloat16 [2048, 4096], P('ctx', 'head')
The draws below stay inside these ranges and needn't reach their ends.
Inputs may be any that keep to these rules, and one draw needn't show every extreme that they name: `random_blocks`: with the blocks i * 4 to i * 4 + 3 called range i: the 12 entries of the rows of range i name blocks of any one range at most 1 times, and some range exactly 1 times. `global_blocks`: 4 different blocks, one of them the last block 63, in any order.
All inputs are finite; a program needn't handle non-finite values.
Results may differ from the reference program's by a relative error of at most 0.0077.
Values may be sent and summed in bfloat16 or wider, within the bound.
A program may use at most 128 MiB of HBM per device.

```python
import math
import jax
import jax.numpy as jnp
from jax import lax

HEADS = 32
DH = 128
BS = 32
NR = 3
NG = 4
SEQ = 2048
NB = 64
BQ = 4
N_CTX = 16


def base_field(key):
    return jnp.clip(jax.random.normal(key, (SEQ, HEADS * DH), dtype=jnp.float32), -4.6, 4.6)


def draw_queries(key, part):
    values = base_field(jax.random.fold_in(key, 1))
    return values.astype(jnp.bfloat16)


def draw_key_states(key, part):
    values = base_field(jax.random.fold_in(key, 2))
    return values.astype(jnp.bfloat16)


def one_order(subkey):
    return jax.random.permutation(subkey, N_CTX)


def draw_random_blocks(key, part):
    row_width = BQ * NR
    key_list = jax.random.split(jax.random.fold_in(key, 3), N_CTX)
    orders = jax.vmap(one_order)(key_list)
    chosen = jnp.arange(row_width) % N_CTX
    owners = orders[:, chosen]
    offsets = jax.random.randint(jax.random.fold_in(key, 4), (N_CTX, row_width), 0, BQ)
    return (owners * BQ + offsets).astype(jnp.int32).reshape(NB, NR)


def draw_global_blocks(key, part):
    others = jax.random.permutation(jax.random.fold_in(key, 5), NB - 1)[:NG - 1].astype(jnp.int32)
    chosen = jnp.concatenate([jnp.full((1,), NB - 1, jnp.int32), others])
    order = jax.random.permutation(jax.random.fold_in(key, 6), NG)
    return chosen[order].astype(jnp.int32)


def level_of(rng, shape, pieces, smallest, top_value):
    def one(position, shards_of):
        steps = jax.random.uniform(jax.random.fold_in(jax.random.fold_in(rng, 6), position), (shards_of,), jnp.float32, smallest / len(pieces), top_value / len(pieces))
        return jnp.repeat(jnp.exp(steps), shape[position] // shards_of).reshape((-1,) + (1,) * (len(shape) - position - 1))

    level = one(*pieces[0])
    for cut in pieces[1:]:
        level = level * one(*cut)
    return level


def normal_values(key, shape, scale, most, pieces=(), kind=jnp.bfloat16):
    factor_of = level_of(key, shape, pieces, -0.22, 0.18) if pieces else 1.0
    values = jax.random.normal(key, shape, jnp.float32) * scale * factor_of
    return jnp.minimum(jnp.maximum(values, -most), most).astype(kind)


def setup_inputs(seed: int = 0) -> dict:
    arg_keys = jax.random.split(jax.random.key(seed), 7)
    return {
        "queries": draw_queries(jax.random.fold_in(arg_keys[6], 71), 0),
        "key_states": draw_key_states(jax.random.fold_in(arg_keys[6], 71), 0),
        "value_states": normal_values(arg_keys[2], (SEQ, HEADS * DH), 1.0, 6.0, ((0, 32),)),
        "out_grad": normal_values(arg_keys[3], (SEQ, HEADS * DH), 1.0, 6.0, ((0, 32),)),
        "random_blocks": draw_random_blocks(jax.random.fold_in(arg_keys[6], 71), 0),
        "global_blocks": draw_global_blocks(jax.random.fold_in(arg_keys[6], 71), 0),
    }


def settle(partial_value):
    middle = partial_value[:, 3:3 + NR]
    rounded = lax.optimization_barrier(middle.astype(jnp.bfloat16)).astype(jnp.float32)
    return jnp.concatenate([partial_value[:, :3], rounded, partial_value[:, 3 + NR:]], axis=1)

def reference(queries, key_states, value_states, out_grad, random_blocks, global_blocks):
    list_len = 3 + NR + NG
    blocks = jnp.arange(NB, dtype=jnp.int32)
    listed = jnp.concatenate([(blocks - 1)[:, None], blocks[:, None], (blocks + 1)[:, None], random_blocks.astype(jnp.int32), jnp.broadcast_to(global_blocks.astype(jnp.int32)[None, :], (NB, NG))], axis=1)
    usable = (listed >= 0) & (listed < NB)
    clipped = jnp.clip(listed, 0, NB - 1).astype(jnp.int32)
    column_ok = jnp.repeat(usable, BS, axis=1)[:, None, :]
    targets = clipped.reshape(-1)
    inv_root = 1.0 / math.sqrt(DH)

    def one_head(unused, head_index):
        offset = head_index * DH

        def columns_of(array):
            return lax.dynamic_slice_in_dim(array, offset, DH, 1).astype(jnp.float32).reshape(NB, BS, DH)
        query_cols = columns_of(queries)
        key_cols = columns_of(key_states)
        value_cols = columns_of(value_states)
        grad_cols = columns_of(out_grad)
        listed_keys = key_cols[clipped]
        listed_values = value_cols[clipped]
        scores = jnp.einsum('nqd,ngkd->nqgk', query_cols, listed_keys).reshape(NB, BS, list_len * BS) * inv_root
        masked = jnp.where(column_ok, scores, -jnp.inf)
        row_max = lax.optimization_barrier(jnp.max(masked, axis=2, keepdims=True))
        log_total = row_max + jnp.log(lax.optimization_barrier(jnp.sum(jnp.exp(masked - row_max), axis=2, keepdims=True)))
        probs_full = jnp.exp(masked - log_total)
        probs_half = lax.optimization_barrier(probs_full.astype(jnp.bfloat16)).astype(jnp.float32)
        probs_four = probs_half.reshape(NB, BS, list_len, BS)
        outputs = jnp.einsum('nqgk,ngkd->nqd', probs_four, listed_values)
        row_dot = lax.optimization_barrier(jnp.sum(grad_cols * outputs, axis=2, keepdims=True))
        dprobs = jnp.einsum('nqd,ngkd->nqgk', grad_cols, listed_values).reshape(NB, BS, list_len * BS)
        dscores = probs_full * (dprobs - row_dot)
        ds_half = lax.optimization_barrier(dscores.astype(jnp.bfloat16)).astype(jnp.float32)
        ds_four = ds_half.reshape(NB, BS, list_len, BS)
        query_grad = jnp.einsum('nqgk,ngkd->nqd', ds_four, listed_keys) * inv_root
        key_part = jnp.einsum('nqgk,nqd->ngkd', ds_four, query_cols) * inv_root
        value_part = jnp.einsum('nqgk,nqd->ngkd', probs_four, grad_cols)
        key_grad = jnp.zeros((NB, BS, DH), jnp.float32).at[targets].add(settle(key_part).reshape(-1, BS, DH))
        value_grad = jnp.zeros((NB, BS, DH), jnp.float32).at[targets].add(settle(value_part).reshape(-1, BS, DH))
        return (unused, (query_grad.reshape(SEQ, DH).astype(jnp.bfloat16), key_grad.reshape(SEQ, DH).astype(jnp.bfloat16), value_grad.reshape(SEQ, DH).astype(jnp.bfloat16)))
    _, (query_all, key_all, value_all) = lax.scan(one_head, jnp.int32(0), jnp.arange(HEADS, dtype=jnp.int32))

    def arrange(stacked):
        return jnp.transpose(stacked, (1, 0, 2)).reshape(SEQ, HEADS * DH)
    return (arrange(query_all), arrange(key_all), arrange(value_all))
```

```python
import functools
import math

import jax
import jax.numpy as jnp
from jax import lax
from jax.experimental import pallas as pl
from jax.experimental.pallas import tpu as pltpu
from jax.sharding import PartitionSpec as P

DH = 128
BS = 32
NR = 3
NG = 4
F32 = jnp.float32
BF16 = jnp.bfloat16


def dot(a, b, dims):
    return lax.dot_general(a, b, (dims, ((), ())), preferred_element_type=F32)


def pick_kernel(idx_ref, x_ref, o_ref):
    o_ref[0] = x_ref[:, 0]


def pick(kv, idx):
    n, cols = idx.shape[0], kv.shape[3]
    return pl.pallas_call(
        pick_kernel,
        out_shape=jax.ShapeDtypeStruct((n, 2, BS, cols), BF16),
        grid_spec=pltpu.PrefetchScalarGridSpec(
            num_scalar_prefetch=1,
            grid=(n,),
            in_specs=[pl.BlockSpec((2, 1, BS, cols), lambda r, idx: (0, idx[r], 0, 0))],
            out_specs=pl.BlockSpec((1, 2, BS, cols), lambda r, idx: (r, 0, 0, 0)),
        ),
    )(idx, kv)


def attend_kernel(
    blocks, heads, sc, qg, kv, before, after, incoming, glob, dq, back, far, own, rim_a, rim_b
):
    inv_root = 1.0 / math.sqrt(DH)
    entries = blocks * NR
    for h in range(heads):
        c = slice(h * DH, (h + 1) * DH)
        back[:, :, :, c] = jnp.zeros((back.shape[0], 2, BS, DH), BF16)
        gk = [glob[i, 0, :, c] for i in range(NG)]
        gv = [glob[i, 1, :, c] for i in range(NG)]
        totals = [[None] * blocks, [None] * blocks]
        far_total = [None, None]

        def add(which, m, part):
            old = totals[which][m]
            totals[which][m] = part if old is None else old + part

        for n in range(blocks):
            rows = slice(n * BS, (n + 1) * BS)
            qn, gn = qg[0, rows, c], qg[1, rows, c]

            def listed(w, far_list):
                out = [
                    before[w, :, c] if n == 0 else kv[w, n - 1, :, c],
                    kv[w, n, :, c],
                    after[w, :, c] if n == blocks - 1 else kv[w, n + 1, :, c],
                ]
                out += [incoming[sc[n * NR + j], w, :, c] for j in range(NR)]
                return jnp.concatenate(out + far_list, axis=0)

            kn, vn = listed(0, gk), listed(1, gv)
            s = dot(qn, kn, ((1,), (1,))) * inv_root
            dp = dot(gn, vn, ((1,), (1,)))
            if n == 0 or n == blocks - 1:
                col = lax.broadcasted_iota(jnp.int32, s.shape, 1)
                if n == 0:
                    s = jnp.where(col < sc[entries], -jnp.inf, s)
                if n == blocks - 1:
                    bad = (col >= 2 * BS) & (col < 2 * BS + sc[entries + 1])
                    s = jnp.where(bad, -jnp.inf, s)
            e = jnp.exp(s - jnp.max(s, axis=1, keepdims=True))
            p = e / jnp.sum(e, axis=1, keepdims=True)
            ph = p.astype(BF16)
            row_dot = jnp.sum(ph.astype(F32) * dp, axis=1, keepdims=True)
            ds = (p * (dp - row_dot)).astype(BF16)
            dq[rows, c] = (dot(ds, kn, ((1,), (0,))) * inv_root).astype(BF16)
            for w, part in (
                (0, dot(ds, qn, ((0,), (0,))) * inv_root),
                (1, dot(ph, gn, ((0,), (0,)))),
            ):
                if n == 0:
                    rim_a[w, :, c] = part[:BS].astype(BF16)
                else:
                    add(w, n - 1, part[:BS])
                add(w, n, part[BS : 2 * BS])
                if n == blocks - 1:
                    rim_b[w, :, c] = part[2 * BS : 3 * BS].astype(BF16)
                else:
                    add(w, n + 1, part[2 * BS : 3 * BS])
                for j in range(NR):
                    piece = part[(3 + j) * BS : (4 + j) * BS].astype(BF16)
                    back[sc[n * NR + j], w, :, c] = piece
                tail = part[(3 + NR) * BS :]
                far_total[w] = tail if far_total[w] is None else far_total[w] + tail
        for w in range(2):
            for m in range(blocks):
                own[w, m, :, c] = totals[w][m]
            for i in range(NG):
                far[i, w, :, c] = far_total[w][i * BS : (i + 1) * BS].astype(BF16)


def finish_kernel(blocks, devices, sc, own, arrived, far, rim_a, rim_b, dk, dv, acc):
    acc[...] = own[...]
    acc[:, 0] += rim_a[...].astype(F32)
    acc[:, blocks - 1] += rim_b[...].astype(F32)
    for r in range(devices):
        @pl.when(sc[r] < blocks)
        def _():
            acc[:, sc[r]] += arrived[r].astype(F32)
    for g in range(NG):
        @pl.when(sc[devices + g] < blocks)
        def _():
            acc[:, sc[devices + g]] += far[g].astype(F32)
    for w, out in ((0, dk), (1, dv)):
        for m in range(blocks):
            out[m * BS : (m + 1) * BS, :] = acc[w, m].astype(BF16)


def columns(shape, cols):
    lead = (0,) * (len(shape) - 1)
    return pl.BlockSpec(tuple(shape[:-1]) + (cols,), lambda i, *_: lead + (i,))


def by_columns(kernel, scalars, arrays, outs, cols, scratch=()):
    steps = arrays[0].shape[-1] // cols
    return pl.pallas_call(
        kernel,
        out_shape=outs,
        grid_spec=pltpu.PrefetchScalarGridSpec(
            num_scalar_prefetch=1,
            grid=(steps,),
            in_specs=[columns(a.shape, cols) for a in arrays],
            out_specs=[columns(o.shape, cols) for o in outs],
            scratch_shapes=scratch,
        ),
        compiler_params=pltpu.CompilerParams(vmem_limit_bytes=40 * 2**20),
    )(scalars, *arrays)


def to_heads(x, y):
    return lax.all_to_all(jnp.stack([x, y]), "head", split_axis=2, concat_axis=1, tiled=True)


def exchange(x):
    return lax.all_to_all(x, "ctx", split_axis=0, concat_axis=0, tiled=True)


def per_device(queries, key_states, value_states, out_grad, random_blocks, global_blocks):
    kv = to_heads(key_states, value_states)
    qg = to_heads(queries, out_grad)
    tokens, cols = kv.shape[1:]
    blocks = tokens // BS
    devices = lax.axis_size("ctx")
    me = lax.axis_index("ctx")
    entries = blocks * NR
    up = [(i, i + 1) for i in range(devices - 1)]
    down = [(j, i) for i, j in up]
    kv = kv.reshape(2, blocks, BS, cols)

    table = random_blocks.reshape(devices, entries)
    served = table // blocks == me
    served_block = jnp.sum(jnp.where(served, table % blocks, 0), axis=1)
    served_used = jnp.any(served, axis=1)
    my_owner = lax.dynamic_index_in_dim(table, me, 0, keepdims=False) // blocks
    global_owner = global_blocks // blocks
    global_offset = global_blocks % blocks
    edge = jnp.stack([jnp.where(me == 0, BS, 0), jnp.where(me == devices - 1, BS, 0)])
    attend_scalars = jnp.concatenate([my_owner, edge]).astype(jnp.int32)
    finish_scalars = jnp.concatenate(
        [
            jnp.where(served_used, served_block, blocks),
            jnp.where(global_owner == me, global_offset, blocks),
        ]
    ).astype(jnp.int32)

    rows = NG * 2 * BS // devices
    pieces = exchange(pick(kv, global_offset).reshape(devices, rows, cols))
    source = jnp.take(global_owner, me * NG // devices)
    piece = lax.dynamic_index_in_dim(pieces, source, 0, keepdims=True)
    glob = exchange(jnp.broadcast_to(piece, (devices, rows, cols))).reshape(NG, 2, BS, cols)
    incoming = exchange(pick(kv, served_block))
    before = lax.ppermute(kv[:, blocks - 1], "ctx", up)
    after = lax.ppermute(kv[:, 0], "ctx", down)

    width = 2 * DH if cols % (2 * DH) == 0 else DH
    shape = jax.ShapeDtypeStruct
    dq, back, far, own, rim_a, rim_b = by_columns(
        functools.partial(attend_kernel, blocks, width // DH),
        attend_scalars,
        [qg, kv, before, after, incoming, glob],
        [
            shape((tokens, cols), BF16),
            shape((devices, 2, BS, cols), BF16),
            shape((NG, 2, BS, cols), BF16),
            shape((2, blocks, BS, cols), F32),
            shape((2, BS, cols), BF16),
            shape((2, BS, cols), BF16),
        ],
        width,
    )

    far_parts = exchange(far.reshape(devices, rows, cols))
    far_piece = jnp.sum(far_parts.astype(F32), axis=0, keepdims=True).astype(BF16)
    arrived = exchange(back)
    far_sum = exchange(jnp.broadcast_to(far_piece, (devices, rows, cols))).reshape(NG, 2, BS, cols)
    from_next = lax.ppermute(rim_a, "ctx", down)
    from_last = lax.ppermute(rim_b, "ctx", up)
    dk, dv = by_columns(
        functools.partial(finish_kernel, blocks, devices),
        finish_scalars,
        [own, arrived, far_sum, from_last, from_next],
        [shape((tokens, cols), BF16)] * 2,
        width,
        [pltpu.VMEM((2, blocks, BS, width), F32)],
    )
    return dq, dk, dv


def solution(mesh):
    placed = P(("ctx", "head"), None)
    return jax.shard_map(
        per_device,
        mesh=mesh,
        in_specs=(placed, placed, placed, placed, P(), P()),
        out_specs=(P("ctx", "head"), P("ctx", "head"), P("ctx", "head")),
        check_vma=False,
    )
```

```python
import functools
import math

import jax
import jax.numpy as jnp
from jax import lax
from jax.experimental import pallas as pl
from jax.experimental.pallas import tpu as pltpu
from jax.sharding import PartitionSpec as P

DH = 128
BS = 32
NR = 3
NG = 4
F32 = jnp.float32
BF16 = jnp.bfloat16


def dot(a, b, dims):
    return lax.dot_general(a, b, (dims, ((), ())), preferred_element_type=F32)


def pick_kernel(idx_ref, x_ref, o_ref):
    o_ref[0] = x_ref[:, 0]


def pick(kv, idx):
    n, cols = idx.shape[0], kv.shape[3]
    return pl.pallas_call(
        pick_kernel,
        out_shape=jax.ShapeDtypeStruct((n, 2, BS, cols), BF16),
        grid_spec=pltpu.PrefetchScalarGridSpec(
            num_scalar_prefetch=1,
            grid=(n,),
            in_specs=[pl.BlockSpec((2, 1, BS, cols), lambda r, idx: (0, idx[r], 0, 0))],
            out_specs=pl.BlockSpec((1, 2, BS, cols), lambda r, idx: (r, 0, 0, 0)),
        ),
    )(idx, kv)


def attend_kernel(
    blocks, heads, sc, qg, kv, before, after, incoming, glob, dq, back, far, own, rim_a, rim_b
):
    inv_root = 1.0 / math.sqrt(DH)
    entries = blocks * NR
    for h in range(heads):
        c = slice(h * DH, (h + 1) * DH)
        back[:, :, :, c] = jnp.zeros((back.shape[0], 2, BS, DH), BF16)
        gk = [glob[i, 0, :, c] for i in range(NG)]
        gv = [glob[i, 1, :, c] for i in range(NG)]
        totals = [[None] * blocks, [None] * blocks]
        far_total = [None, None]

        def add(which, m, part):
            old = totals[which][m]
            totals[which][m] = part if old is None else old + part

        for n in range(blocks):
            rows = slice(n * BS, (n + 1) * BS)
            qn, gn = qg[0, rows, c], qg[1, rows, c]

            def listed(w, far_list):
                out = [
                    before[w, :, c] if n == 0 else kv[w, n - 1, :, c],
                    kv[w, n, :, c],
                    after[w, :, c] if n == blocks - 1 else kv[w, n + 1, :, c],
                ]
                out += [incoming[sc[n * NR + j], w, :, c] for j in range(NR)]
                return jnp.concatenate(out + far_list, axis=0)

            kn, vn = listed(0, gk), listed(1, gv)
            s = dot(qn, kn, ((1,), (1,))) * inv_root
            dp = dot(gn, vn, ((1,), (1,)))
            if n == 0 or n == blocks - 1:
                col = lax.broadcasted_iota(jnp.int32, s.shape, 1)
                if n == 0:
                    s = jnp.where(col < sc[entries], -jnp.inf, s)
                if n == blocks - 1:
                    bad = (col >= 2 * BS) & (col < 2 * BS + sc[entries + 1])
                    s = jnp.where(bad, -jnp.inf, s)
            e = jnp.exp(s - jnp.max(s, axis=1, keepdims=True))
            p = e / jnp.sum(e, axis=1, keepdims=True)
            ph = p.astype(BF16)
            row_dot = jnp.sum(ph.astype(F32) * dp, axis=1, keepdims=True)
            ds = (p * (dp - row_dot)).astype(BF16)
            dq[rows, c] = (dot(ds, kn, ((1,), (0,))) * inv_root).astype(BF16)
            for w, part in (
                (0, dot(ds, qn, ((0,), (0,))) * inv_root),
                (1, dot(ph, gn, ((0,), (0,)))),
            ):
                if n == 0:
                    rim_a[w, :, c] = part[:BS].astype(BF16)
                else:
                    add(w, n - 1, part[:BS])
                add(w, n, part[BS : 2 * BS])
                if n == blocks - 1:
                    rim_b[w, :, c] = part[2 * BS : 3 * BS].astype(BF16)
                else:
                    add(w, n + 1, part[2 * BS : 3 * BS])
                for j in range(NR):
                    piece = part[(3 + j) * BS : (4 + j) * BS].astype(BF16)
                    back[sc[n * NR + j], w, :, c] = piece
                tail = part[(3 + NR) * BS :]
                far_total[w] = tail if far_total[w] is None else far_total[w] + tail
        for w in range(2):
            for m in range(blocks):
                own[w, m, :, c] = totals[w][m]
            for i in range(NG):
                far[i, w, :, c] = far_total[w][i * BS : (i + 1) * BS].astype(BF16)


def finish_kernel(blocks, devices, sc, own, arrived, far, rim_a, rim_b, dk, dv, acc):
    acc[...] = own[...]
    acc[:, 0] += rim_a[...].astype(F32)
    acc[:, blocks - 1] += rim_b[...].astype(F32)
    for r in range(devices):
        @pl.when(sc[r] < blocks)
        def _():
            acc[:, sc[r]] += arrived[r].astype(F32)
    for g in range(NG):
        @pl.when(sc[devices + g] < blocks)
        def _():
            acc[:, sc[devices + g]] += far[g].astype(F32)
    for w, out in ((0, dk), (1, dv)):
        for m in range(blocks):
            out[m * BS : (m + 1) * BS, :] = acc[w, m].astype(BF16)


def columns(shape, cols):
    lead = (0,) * (len(shape) - 1)
    return pl.BlockSpec(tuple(shape[:-1]) + (cols,), lambda i, *_: lead + (i,))


def by_columns(kernel, scalars, arrays, outs, cols, scratch=()):
    steps = arrays[0].shape[-1] // cols
    return pl.pallas_call(
        kernel,
        out_shape=outs,
        grid_spec=pltpu.PrefetchScalarGridSpec(
            num_scalar_prefetch=1,
            grid=(steps,),
            in_specs=[columns(a.shape, cols) for a in arrays],
            out_specs=[columns(o.shape, cols) for o in outs],
            scratch_shapes=scratch,
        ),
        compiler_params=pltpu.CompilerParams(vmem_limit_bytes=40 * 2**20),
    )(scalars, *arrays)


MESH = pl.DeviceIdType.MESH
ANY = pl.BlockSpec(memory_space=pl.ANY)
VMEM = pl.BlockSpec(memory_space=pltpu.VMEM)
SMEM = pl.BlockSpec(memory_space=pltpu.SMEM)


def others(axis, n, body, first=1, last=None):
    me = lax.axis_index(axis)

    def step(d, carry):
        body(lax.rem(me + d, n))
        return carry

    lax.fori_loop(first, n if last is None else last, step, 0)


def meet(axes):
    barrier = pltpu.get_barrier_semaphore()
    for axis, n in axes:
        others(axis, n, lambda p: pl.semaphore_signal(
            barrier, inc=1, device_id={axis: p}, device_id_type=MESH))
    pl.semaphore_wait(barrier, sum(n - 1 for _, n in axes))


def head_exchange(n, xs, out, send, recv, local):
    me = lax.axis_index("head")
    rows, cols = xs[0].shape[0], out.shape[2]

    def copy(i, p):
        return pltpu.make_async_remote_copy(
            src_ref=xs[i].at[:, pl.ds(pl.multiple_of(p * cols, DH), cols)],
            dst_ref=out.at[i, pl.ds(pl.multiple_of(me * rows, rows), rows)],
            send_sem=send.at[i, p],
            recv_sem=recv.at[i, me],
            device_id={"head": p},
            device_id_type=MESH,
        )

    def arrival(i, p):
        return pltpu.make_async_remote_copy(
            src_ref=xs[i].at[:, pl.ds(pl.multiple_of(p * cols, DH), cols)],
            dst_ref=out.at[i, pl.ds(pl.multiple_of(p * rows, rows), rows)],
            send_sem=send.at[i, p],
            recv_sem=recv.at[i, p],
            device_id={"head": p},
            device_id_type=MESH,
        )

    def own(i):
        return pltpu.make_async_copy(
            xs[i].at[:, pl.ds(pl.multiple_of(me * cols, DH), cols)],
            out.at[i, pl.ds(pl.multiple_of(me * rows, rows), rows)],
            local.at[i],
        )

    for i in range(2):
        others("head", n, lambda p: copy(i, p).start())
        own(i).start()

    def wait():
        for i in range(2):
            others("head", n, lambda p: arrival(i, p).wait())
            own(i).wait()

    return wait


def heads_kernel(n, x, y, out, send, recv, local):
    meet([("head", n)])
    head_exchange(n, (x, y), out, send, recv, local)()


def head_sems(n):
    return [
        pltpu.SemaphoreType.DMA((2, n)),
        pltpu.SemaphoreType.DMA((2, n)),
        pltpu.SemaphoreType.DMA((2,)),
    ]


def to_heads(x, y):
    n = lax.axis_size("head")
    rows, cols = x.shape
    return pl.pallas_call(
        functools.partial(heads_kernel, n),
        out_shape=jax.ShapeDtypeStruct((2, rows * n, cols // n), BF16),
        in_specs=[ANY, ANY],
        out_specs=ANY,
        scratch_shapes=head_sems(n),
        compiler_params=pltpu.CompilerParams(collective_id=0, has_side_effects=True),
    )(x, y)


def all_to_all(n, src, dst, send, recv, local):
    me = lax.axis_index("ctx")

    def copy(slot, p):
        return pltpu.make_async_remote_copy(
            src_ref=src(p),
            dst_ref=dst.at[slot],
            send_sem=send.at[p],
            recv_sem=recv.at[slot],
            device_id={"ctx": p},
            device_id_type=MESH,
        )

    own = pltpu.make_async_copy(src(me), dst.at[me], local)

    def start(first=1, last=None):
        others("ctx", n, lambda p: copy(me, p).start(), first, last)
        if first == 1:
            own.start()

    def wait():
        others("ctx", n, lambda p: copy(p, p).wait())
        own.wait()

    return start, wait


def trade_kernel(n, hn, source, parts, blocks, to_next, to_last, *refs):
    forward = hn > 0
    if forward:
        q, g, parts_out, blocks_out, from_last, from_next, qg = refs[:7]
        refs = refs[7:]
    else:
        parts_out, blocks_out, from_last, from_next = refs[:4]
        refs = refs[4:]
    got, piece, s1, r1, s2, r2, s3, r3, s4, r4, local = refs[:11]
    me = lax.axis_index("ctx")
    after, before = lax.rem(me + 1, n), lax.rem(me + n - 1, n)
    meet([("ctx", n)] + ([("head", hn)] if forward else []))
    start1, wait1 = all_to_all(n, lambda p: parts.at[p], got, s1, r1, local.at[0])
    start2, wait2 = all_to_all(n, lambda p: piece, parts_out, s2, r2, local.at[1])
    start3, wait3 = all_to_all(n, lambda p: blocks.at[p], blocks_out, s3, r3, local.at[2])
    start1()
    if forward:
        wait_heads = head_exchange(hn, (q, g), qg, *refs[11:])
    edges = [
        pltpu.make_async_remote_copy(
            src_ref=a,
            dst_ref=b,
            send_sem=s4.at[i],
            recv_sem=r4.at[i],
            device_id={"ctx": p},
            device_id_type=MESH,
        )
        for i, (a, b, p) in enumerate([(to_next, from_last, after), (to_last, from_next, before)])
    ]
    for e in edges:
        e.start()
    start3(1, n // 4)
    wait1()
    if forward:
        piece[...] = got[source[0]]
    else:
        total = lax.fori_loop(
            0, n, lambda i, t: t + got[i].astype(F32), jnp.zeros(piece.shape, F32)
        )
        piece[...] = total.astype(BF16)
    start2()
    start3(n // 4)
    wait2()
    for e in edges:
        e.wait()
    wait3()
    if forward:
        wait_heads()


def trade(source, parts, blocks, to_next, to_last, queries=()):
    n = lax.axis_size("ctx")
    hn = lax.axis_size("head") if queries else 0
    dma = pltpu.SemaphoreType.DMA
    outs = [jax.ShapeDtypeStruct(a.shape, BF16) for a in (parts, blocks, to_next, to_last)]
    if queries:
        rows, cols = queries[0].shape
        outs.append(jax.ShapeDtypeStruct((2, rows * hn, cols // hn), BF16))
    return pl.pallas_call(
        functools.partial(trade_kernel, n, hn),
        out_shape=outs,
        in_specs=[SMEM, VMEM] + [ANY] * (3 + len(queries)),
        out_specs=[ANY] * len(outs),
        scratch_shapes=[
            pltpu.VMEM(parts.shape, BF16),
            pltpu.VMEM(parts.shape[1:], BF16),
            *[dma((n,))] * 6,
            dma((2,)),
            dma((2,)),
            dma((3,)),
            *(head_sems(hn) if queries else []),
        ],
        compiler_params=pltpu.CompilerParams(
            collective_id=1 if queries else 2, has_side_effects=True
        ),
    )(source, parts, blocks, to_next, to_last, *queries)


def per_device(queries, key_states, value_states, out_grad, random_blocks, global_blocks):
    kv = to_heads(key_states, value_states)
    tokens, cols = kv.shape[1:]
    blocks = tokens // BS
    devices = lax.axis_size("ctx")
    me = lax.axis_index("ctx")
    entries = blocks * NR
    kv = kv.reshape(2, blocks, BS, cols)

    table = random_blocks.reshape(devices, entries)
    served = table // blocks == me
    served_block = jnp.sum(jnp.where(served, table % blocks, 0), axis=1)
    served_used = jnp.any(served, axis=1)
    my_owner = lax.dynamic_index_in_dim(table, me, 0, keepdims=False) // blocks
    global_owner = global_blocks // blocks
    global_offset = global_blocks % blocks
    edge = jnp.stack([jnp.where(me == 0, BS, 0), jnp.where(me == devices - 1, BS, 0)])
    attend_scalars = jnp.concatenate([my_owner, edge]).astype(jnp.int32)
    finish_scalars = jnp.concatenate(
        [
            jnp.where(served_used, served_block, blocks),
            jnp.where(global_owner == me, global_offset, blocks),
        ]
    ).astype(jnp.int32)

    rows = NG * 2 * BS // devices
    source = jnp.take(global_owner, me * NG // devices).reshape(1)
    glob, incoming, before, after, qg = trade(
        source,
        pick(kv, global_offset).reshape(devices, rows, cols),
        pick(kv, served_block),
        kv[:, blocks - 1],
        kv[:, 0],
        (queries, out_grad),
    )
    glob = glob.reshape(NG, 2, BS, cols)

    width = 2 * DH if cols % (2 * DH) == 0 else DH
    shape = jax.ShapeDtypeStruct
    dq, back, far, own, rim_a, rim_b = by_columns(
        functools.partial(attend_kernel, blocks, width // DH),
        attend_scalars,
        [qg, kv, before, after, incoming, glob],
        [
            shape((tokens, cols), BF16),
            shape((devices, 2, BS, cols), BF16),
            shape((NG, 2, BS, cols), BF16),
            shape((2, blocks, BS, cols), F32),
            shape((2, BS, cols), BF16),
            shape((2, BS, cols), BF16),
        ],
        width,
    )

    far_sum, arrived, from_last, from_next = trade(
        source, far.reshape(devices, rows, cols), back, rim_b, rim_a
    )
    far_sum = far_sum.reshape(NG, 2, BS, cols)
    dk, dv = by_columns(
        functools.partial(finish_kernel, blocks, devices),
        finish_scalars,
        [own, arrived, far_sum, from_last, from_next],
        [shape((tokens, cols), BF16)] * 2,
        width,
        [pltpu.VMEM((2, blocks, BS, width), F32)],
    )
    return dq, dk, dv


def solution(mesh):
    placed = P(("ctx", "head"), None)
    return jax.shard_map(
        per_device,
        mesh=mesh,
        in_specs=(placed, placed, placed, placed, P(), P()),
        out_specs=(P("ctx", "head"), P("ctx", "head"), P("ctx", "head")),
        check_vma=False,
    )
```

```python
import functools
import math

import jax
import jax.numpy as jnp
from jax import lax
from jax.experimental import pallas as pl
from jax.experimental.pallas import tpu as pltpu
from jax.sharding import PartitionSpec as P

DH = 128
BS = 32
NR = 3
NG = 4
F32 = jnp.float32
BF16 = jnp.bfloat16


def dot(a, b, dims):
    return lax.dot_general(a, b, (dims, ((), ())), preferred_element_type=F32)


def attend_kernel(
    blocks, heads, sc, qg, kv, dq, back, far, own, rim_a, rim_b
):
    inv_root = 1.0 / math.sqrt(DH)
    entries = blocks * NR
    for h in range(heads):
        c = slice(h * DH, (h + 1) * DH)
        back[:, :, :, c] = jnp.zeros((back.shape[0], 2, BS, DH), BF16)
        gk, gv = ([kv[w, sc[2 * entries + 3 + i], :, c] for i in range(NG)] for w in range(2))
        first, final = sc[2 * entries + 2], kv.shape[1] - 1
        totals = [[None] * blocks, [None] * blocks]
        far_total = [None, None]

        def add(which, m, part):
            old = totals[which][m]
            totals[which][m] = part if old is None else old + part

        for n in range(blocks):
            rows = slice(n * BS, (n + 1) * BS)
            qn, gn = qg[0, rows, c], qg[1, rows, c]

            def listed(w, far_list):
                at = [jnp.maximum(first + n - 1, 0), first + n, jnp.minimum(first + n + 1, final)]
                at += [sc[entries + 2 + n * NR + j] for j in range(NR)]
                out = [kv[w, m, :, c] for m in at]
                return jnp.concatenate(out + far_list, axis=0)

            kn, vn = listed(0, gk), listed(1, gv)
            s = dot(qn, kn, ((1,), (1,))) * inv_root
            dp = dot(gn, vn, ((1,), (1,)))
            if n == 0 or n == blocks - 1:
                col = lax.broadcasted_iota(jnp.int32, s.shape, 1)
                if n == 0:
                    s = jnp.where(col < sc[entries], -jnp.inf, s)
                if n == blocks - 1:
                    bad = (col >= 2 * BS) & (col < 2 * BS + sc[entries + 1])
                    s = jnp.where(bad, -jnp.inf, s)
            e = jnp.exp(s - jnp.max(s, axis=1, keepdims=True))
            p = e / jnp.sum(e, axis=1, keepdims=True)
            ph = p.astype(BF16)
            row_dot = jnp.sum(ph.astype(F32) * dp, axis=1, keepdims=True)
            ds = (p * (dp - row_dot)).astype(BF16)
            dq[rows, c] = (dot(ds, kn, ((1,), (0,))) * inv_root).astype(BF16)
            for w, part in (
                (0, dot(ds, qn, ((0,), (0,))) * inv_root),
                (1, dot(ph, gn, ((0,), (0,)))),
            ):
                if n == 0:
                    rim_a[w, :, c] = part[:BS].astype(BF16)
                else:
                    add(w, n - 1, part[:BS])
                add(w, n, part[BS : 2 * BS])
                if n == blocks - 1:
                    rim_b[w, :, c] = part[2 * BS : 3 * BS].astype(BF16)
                else:
                    add(w, n + 1, part[2 * BS : 3 * BS])
                for j in range(NR):
                    piece = part[(3 + j) * BS : (4 + j) * BS].astype(BF16)
                    back[sc[n * NR + j], w, :, c] = piece
                tail = part[(3 + NR) * BS :]
                far_total[w] = tail if far_total[w] is None else far_total[w] + tail
        for w in range(2):
            for m in range(blocks):
                own[w, m, :, c] = totals[w][m]
            for i in range(NG):
                far[i, w, :, c] = far_total[w][i * BS : (i + 1) * BS].astype(BF16)


def finish_kernel(blocks, devices, sc, own, arrived, far, rim_a, rim_b, dk, dv, acc):
    acc[...] = own[...]
    acc[:, 0] += rim_a[...].astype(F32)
    acc[:, blocks - 1] += rim_b[...].astype(F32)
    for r in range(devices):
        @pl.when(sc[r] < blocks)
        def _():
            acc[:, sc[r]] += arrived[r].astype(F32)
    for g in range(NG):
        @pl.when(sc[devices + g] < blocks)
        def _():
            acc[:, sc[devices + g]] += far[g].astype(F32)
    for w, out in ((0, dk), (1, dv)):
        for m in range(blocks):
            out[m * BS : (m + 1) * BS, :] = acc[w, m].astype(BF16)


def columns(shape, cols):
    lead = (0,) * (len(shape) - 1)
    return pl.BlockSpec(tuple(shape[:-1]) + (cols,), lambda i, *_: lead + (i,))


def by_columns(kernel, scalars, arrays, outs, cols, scratch=()):
    steps = arrays[0].shape[-1] // cols
    return pl.pallas_call(
        kernel,
        out_shape=outs,
        grid_spec=pltpu.PrefetchScalarGridSpec(
            num_scalar_prefetch=1,
            grid=(steps,),
            in_specs=[columns(a.shape, cols) for a in arrays],
            out_specs=[columns(o.shape, cols) for o in outs],
            scratch_shapes=scratch,
        ),
        compiler_params=pltpu.CompilerParams(vmem_limit_bytes=40 * 2**20),
    )(scalars, *arrays)


MESH = pl.DeviceIdType.MESH
ANY = pl.BlockSpec(memory_space=pl.ANY)
VMEM = pl.BlockSpec(memory_space=pltpu.VMEM)
SMEM = pl.BlockSpec(memory_space=pltpu.SMEM)


def others(axis, n, body, first=1, last=None):
    me = lax.axis_index(axis)

    def step(d, carry):
        body(lax.rem(me + d, n))
        return carry

    lax.fori_loop(first, n if last is None else last, step, 0)


def meet(axes):
    barrier = pltpu.get_barrier_semaphore()
    for axis, n in axes:
        others(axis, n, lambda p: pl.semaphore_signal(
            barrier, inc=1, device_id={axis: p}, device_id_type=MESH))
    pl.semaphore_wait(barrier, sum(n - 1 for _, n in axes))


def head_exchange(n, xs, out, send, recv, local):
    me = lax.axis_index("head")
    rows, cols = xs[0].shape[0], out.shape[2]

    def copy(i, p):
        return pltpu.make_async_remote_copy(
            src_ref=xs[i].at[:, pl.ds(pl.multiple_of(p * cols, DH), cols)],
            dst_ref=out.at[i, pl.ds(pl.multiple_of(me * rows, rows), rows)],
            send_sem=send.at[i, p],
            recv_sem=recv.at[i, me],
            device_id={"head": p},
            device_id_type=MESH,
        )

    def arrival(i, p):
        return pltpu.make_async_remote_copy(
            src_ref=xs[i].at[:, pl.ds(pl.multiple_of(p * cols, DH), cols)],
            dst_ref=out.at[i, pl.ds(pl.multiple_of(p * rows, rows), rows)],
            send_sem=send.at[i, p],
            recv_sem=recv.at[i, p],
            device_id={"head": p},
            device_id_type=MESH,
        )

    def own(i):
        return pltpu.make_async_copy(
            xs[i].at[:, pl.ds(pl.multiple_of(me * cols, DH), cols)],
            out.at[i, pl.ds(pl.multiple_of(me * rows, rows), rows)],
            local.at[i],
        )

    for i in range(2):
        others("head", n, lambda p: copy(i, p).start())
        own(i).start()

    def wait():
        for i in range(2):
            others("head", n, lambda p: arrival(i, p).wait())
            own(i).wait()

    return wait


def head_sems(n):
    return [
        pltpu.SemaphoreType.DMA((2, n)),
        pltpu.SemaphoreType.DMA((2, n)),
        pltpu.SemaphoreType.DMA((2,)),
    ]


def grid_of(n):
    return (n // 4, 2, 2) if n == 16 else (n // 4, 4, 1)


def gather_kernel(n, hn, k, v, q, g, kv, qg, send, recv, *sems):
    nz, ny, nc = grid_of(n)
    me = lax.axis_index("ctx")
    z, y, c = me // (ny * nc), (me // nc) % ny, me % nc

    def at(z, y, c):
        return (z * ny + y) * nc + c

    def copy(w, shard, peer, way):
        return pltpu.make_async_remote_copy(
            src_ref=kv.at[w, shard],
            dst_ref=kv.at[w, shard],
            send_sem=send.at[w, shard, way],
            recv_sem=recv.at[w, shard],
            device_id={"ctx": peer},
            device_id_type=MESH,
        )

    def across(w, shard):
        return [copy(w, shard, at(z, lax.rem(y + d, ny), c), 1 + d) for d in range(1, ny)]

    def inside(w, shard):
        return [copy(w, shard, at(z, y, lax.rem(c + d, nc)), 1 + ny - 1 + d) for d in range(1, nc)]

    def along(w, shard, up):
        return copy(w, shard, at(z + 1 if up else z - 1, y, c), 0 if up else 1)

    def has_next(up):
        return z + 1 < nz if up else z > 0

    def every_send(do):
        for dist in range(nz):
            for up in (True, False):
                far = z - dist if up else z + dist

                @pl.when((far >= 0) if up else (far < nz))
                def _():
                    for d in range(ny):
                        yy = lax.rem(y + d, ny)
                        shard = at(far, yy, c)
                        if d == 0:
                            do(0, shard, dist, up, True, up or dist > 0)
                        do(1, shard, dist, up, False, up or dist > 0, d)

            for up in (True, False):
                far = z - dist if up else z + dist
                if dist == 0 and not up:
                    continue

                @pl.when((far >= 0) if up else (far < nz))
                def _():
                    for d in range(1, ny):
                        do(0, at(far, lax.rem(y + d, ny), c), dist, None, False, True, d)

    def start(w, shard, dist, up, cross, once, d=0):
        if once and (dist > 0 or d > 0):
            copy(w, shard, at(z, y, c), 0).wait_recv()
        if up is not None:

            @pl.when(has_next(up))
            def _():
                along(w, shard, up).start()

        if once:
            own_line = w == 0 and cross
            own_shard = w == 1 and dist == 0 and d == 0
            for e in (across(w, shard) if own_line or own_shard else []) + inside(w, shard):
                e.start()

    def finish(w, shard, dist, up, cross, once, d=0):
        if up is not None:

            @pl.when(has_next(up))
            def _():
                along(w, shard, up).wait_send()

        if once:
            own_line = w == 0 and cross
            own_shard = w == 1 and dist == 0 and d == 0
            for e in (across(w, shard) if own_line or own_shard else []) + inside(w, shard):
                e.wait_send()

    meet([("ctx", n), ("head", hn)])
    head_exchange(hn, (k, v), kv.at[:, me], *sems[:3])()
    wait_heads = head_exchange(hn, (q, g), qg, *sems[3:])
    every_send(start)
    for d in range(1, nc):
        cc = lax.rem(c + d, nc)

        def arrive(i, carry):
            for w in range(2):
                copy(w, i * nc + cc, at(z, y, c), 0).wait_recv()
            return carry

        lax.fori_loop(0, nz * ny, arrive, 0)
    every_send(finish)
    wait_heads()


def gather(k, v, q, g):
    n, hn = lax.axis_size("ctx"), lax.axis_size("head")
    _, ny, nc = grid_of(n)
    rows, cols = k.shape[0] * hn, k.shape[1] // hn
    return pl.pallas_call(
        functools.partial(gather_kernel, n, hn),
        out_shape=[
            jax.ShapeDtypeStruct((2, n, rows, cols), BF16),
            jax.ShapeDtypeStruct((2, rows, cols), BF16),
        ],
        in_specs=[ANY] * 4,
        out_specs=[ANY] * 2,
        scratch_shapes=[
            pltpu.SemaphoreType.DMA((2, n, ny + nc)),
            pltpu.SemaphoreType.DMA((2, n)),
            *head_sems(hn),
            *head_sems(hn),
        ],
        compiler_params=pltpu.CompilerParams(collective_id=0, has_side_effects=True),
    )(k, v, q, g)


def all_to_all(n, src, dst, send, recv, local):
    me = lax.axis_index("ctx")

    def copy(slot, p):
        return pltpu.make_async_remote_copy(
            src_ref=src(p),
            dst_ref=dst.at[slot],
            send_sem=send.at[p],
            recv_sem=recv.at[slot],
            device_id={"ctx": p},
            device_id_type=MESH,
        )

    own = pltpu.make_async_copy(src(me), dst.at[me], local)

    def start(first=1, last=None):
        others("ctx", n, lambda p: copy(me, p).start(), first, last)
        if first == 1:
            own.start()

    def wait():
        others("ctx", n, lambda p: copy(p, p).wait())
        own.wait()

    return start, wait


def trade_kernel(n, parts, blocks, to_next, to_last, *refs):
    parts_out, blocks_out, from_last, from_next = refs[:4]
    got, piece, s1, r1, s2, r2, s3, r3, s4, r4, local = refs[4:]
    me = lax.axis_index("ctx")
    after, before = lax.rem(me + 1, n), lax.rem(me + n - 1, n)
    meet([("ctx", n)])
    start1, wait1 = all_to_all(n, lambda p: parts.at[p], got, s1, r1, local.at[0])
    start2, wait2 = all_to_all(n, lambda p: piece, parts_out, s2, r2, local.at[1])
    start3, wait3 = all_to_all(n, lambda p: blocks.at[p], blocks_out, s3, r3, local.at[2])
    start1()
    edges = [
        pltpu.make_async_remote_copy(
            src_ref=a,
            dst_ref=b,
            send_sem=s4.at[i],
            recv_sem=r4.at[i],
            device_id={"ctx": p},
            device_id_type=MESH,
        )
        for i, (a, b, p) in enumerate([(to_next, from_last, after), (to_last, from_next, before)])
    ]
    for e in edges:
        e.start()
    start3(1, n // 4)
    wait1()
    total = lax.fori_loop(0, n, lambda i, t: t + got[i].astype(F32), jnp.zeros(piece.shape, F32))
    piece[...] = total.astype(BF16)
    start2()
    start3(n // 4)
    wait2()
    for e in edges:
        e.wait()
    wait3()


def trade(parts, blocks, to_next, to_last):
    n = lax.axis_size("ctx")
    dma = pltpu.SemaphoreType.DMA
    return pl.pallas_call(
        functools.partial(trade_kernel, n),
        out_shape=[jax.ShapeDtypeStruct(a.shape, BF16) for a in (parts, blocks, to_next, to_last)],
        in_specs=[VMEM] + [ANY] * 3,
        out_specs=[ANY] * 4,
        scratch_shapes=[
            pltpu.VMEM(parts.shape, BF16),
            pltpu.VMEM(parts.shape[1:], BF16),
            *[dma((n,))] * 6,
            dma((2,)),
            dma((2,)),
            dma((3,)),
        ],
        compiler_params=pltpu.CompilerParams(collective_id=1, has_side_effects=True),
    )(parts, blocks, to_next, to_last)


def per_device(queries, key_states, value_states, out_grad, random_blocks, global_blocks):
    kv, qg = gather(key_states, value_states, queries, out_grad)
    tokens, cols = kv.shape[2:]
    blocks = tokens // BS
    devices = lax.axis_size("ctx")
    me = lax.axis_index("ctx")
    entries = blocks * NR
    kv = kv.reshape(2, devices * blocks, BS, cols)

    table = random_blocks.reshape(devices, entries)
    served = table // blocks == me
    served_block = jnp.sum(jnp.where(served, table % blocks, 0), axis=1)
    served_used = jnp.any(served, axis=1)
    mine = lax.dynamic_index_in_dim(table, me, 0, keepdims=False)
    global_owner = global_blocks // blocks
    global_offset = global_blocks % blocks
    edge = jnp.stack([jnp.where(me == 0, BS, 0), jnp.where(me == devices - 1, BS, 0)])
    attend_scalars = jnp.concatenate(
        [mine // blocks, edge, mine, (me * blocks)[None], global_blocks]
    ).astype(jnp.int32)
    finish_scalars = jnp.concatenate(
        [
            jnp.where(served_used, served_block, blocks),
            jnp.where(global_owner == me, global_offset, blocks),
        ]
    ).astype(jnp.int32)

    rows = NG * 2 * BS // devices
    width = 2 * DH if cols % (2 * DH) == 0 else DH
    shape = jax.ShapeDtypeStruct
    dq, back, far, own, rim_a, rim_b = by_columns(
        functools.partial(attend_kernel, blocks, width // DH),
        attend_scalars,
        [qg, kv],
        [
            shape((tokens, cols), BF16),
            shape((devices, 2, BS, cols), BF16),
            shape((NG, 2, BS, cols), BF16),
            shape((2, blocks, BS, cols), F32),
            shape((2, BS, cols), BF16),
            shape((2, BS, cols), BF16),
        ],
        width,
    )

    far_sum, arrived, from_last, from_next = trade(
        far.reshape(devices, rows, cols), back, rim_b, rim_a
    )
    far_sum = far_sum.reshape(NG, 2, BS, cols)
    dk, dv = by_columns(
        functools.partial(finish_kernel, blocks, devices),
        finish_scalars,
        [own, arrived, far_sum, from_last, from_next],
        [shape((tokens, cols), BF16)] * 2,
        width,
        [pltpu.VMEM((2, blocks, BS, width), F32)],
    )
    return dq, dk, dv


def solution(mesh):
    placed = P(("ctx", "head"), None)
    return jax.shard_map(
        per_device,
        mesh=mesh,
        in_specs=(placed, placed, placed, placed, P(), P()),
        out_specs=(P("ctx", "head"), P("ctx", "head"), P("ctx", "head")),
        check_vma=False,
    )
```

```python
import functools
import math

import jax
import jax.numpy as jnp
from jax import lax
from jax.experimental import pallas as pl
from jax.experimental.pallas import tpu as pltpu
from jax.sharding import PartitionSpec as P

DH = 128
BS = 32
NR = 3
NG = 4
F32 = jnp.float32
BF16 = jnp.bfloat16


def dot(a, b, dims):
    return lax.dot_general(a, b, (dims, ((), ())), preferred_element_type=F32)


def attend_kernel(
    blocks, heads, sc, qg, kv, dq, back, far, own, rim_a, rim_b
):
    inv_root = 1.0 / math.sqrt(DH)
    entries = blocks * NR
    for h in range(heads):
        c = slice(h * DH, (h + 1) * DH)
        back[:, :, :, c] = jnp.zeros((back.shape[0], 2, BS, DH), BF16)
        gk, gv = ([kv[w, sc[2 * entries + 3 + i], :, c] for i in range(NG)] for w in range(2))
        first, final = sc[2 * entries + 2], kv.shape[1] - 1
        totals = [[None] * blocks, [None] * blocks]
        far_total = [None, None]
        staged, ready = [], []

        def add(which, m, part):
            old = totals[which][m]
            totals[which][m] = part if old is None else old + part

        for n in range(blocks):
            rows = slice(n * BS, (n + 1) * BS)
            qn, gn = qg[0, rows, c], qg[1, rows, c]

            def listed(w, far_list):
                at = [jnp.maximum(first + n - 1, 0), first + n, jnp.minimum(first + n + 1, final)]
                at += [sc[entries + 2 + n * NR + j] for j in range(NR)]
                out = [kv[w, m, :, c] for m in at]
                return jnp.concatenate(out + far_list, axis=0)

            kn, vn = listed(0, gk), listed(1, gv)
            s = dot(qn, kn, ((1,), (1,))) * inv_root
            dp = dot(gn, vn, ((1,), (1,)))
            if n == 0 or n == blocks - 1:
                col = lax.broadcasted_iota(jnp.int32, s.shape, 1)
                if n == 0:
                    s = jnp.where(col < sc[entries], -jnp.inf, s)
                if n == blocks - 1:
                    bad = (col >= 2 * BS) & (col < 2 * BS + sc[entries + 1])
                    s = jnp.where(bad, -jnp.inf, s)
            staged.append((rows, qn, gn, kn, s, dp))

        for n, (rows, qn, gn, kn, s, dp) in enumerate(staged):
            e = jnp.exp(s - jnp.max(s, axis=1, keepdims=True))
            p = e / jnp.sum(e, axis=1, keepdims=True)
            ph = p.astype(BF16)
            row_dot = jnp.sum(ph.astype(F32) * dp, axis=1, keepdims=True)
            ds = (p * (dp - row_dot)).astype(BF16)
            ready.append((rows, qn, gn, kn, ph, ds))

        for n, (rows, qn, gn, kn, ph, ds) in enumerate(ready):
            dq[rows, c] = (dot(ds, kn, ((1,), (0,))) * inv_root).astype(BF16)
            for w, part in (
                (0, dot(ds, qn, ((0,), (0,))) * inv_root),
                (1, dot(ph, gn, ((0,), (0,)))),
            ):
                if n == 0:
                    rim_a[w, :, c] = part[:BS].astype(BF16)
                else:
                    add(w, n - 1, part[:BS])
                add(w, n, part[BS : 2 * BS])
                if n == blocks - 1:
                    rim_b[w, :, c] = part[2 * BS : 3 * BS].astype(BF16)
                else:
                    add(w, n + 1, part[2 * BS : 3 * BS])
                for j in range(NR):
                    piece = part[(3 + j) * BS : (4 + j) * BS].astype(BF16)
                    back[sc[n * NR + j], w, :, c] = piece
                tail = part[(3 + NR) * BS :]
                far_total[w] = tail if far_total[w] is None else far_total[w] + tail
        for w in range(2):
            for m in range(blocks):
                own[w, m, :, c] = totals[w][m]
            for i in range(NG):
                far[i, w, :, c] = far_total[w][i * BS : (i + 1) * BS].astype(BF16)


def finish_kernel(blocks, devices, sc, own, arrived, far, rim_a, rim_b, dk, dv, acc):
    acc[...] = own[...]
    acc[:, 0] += rim_a[...].astype(F32)
    acc[:, blocks - 1] += rim_b[...].astype(F32)
    for r in range(devices):
        @pl.when(sc[r] < blocks)
        def _():
            acc[:, sc[r]] += arrived[r].astype(F32)
    for g in range(NG):
        @pl.when(sc[devices + g] < blocks)
        def _():
            acc[:, sc[devices + g]] += far[g].astype(F32)
    for w, out in ((0, dk), (1, dv)):
        for m in range(blocks):
            out[m * BS : (m + 1) * BS, :] = acc[w, m].astype(BF16)


def columns(shape, cols):
    lead = (0,) * (len(shape) - 1)
    return pl.BlockSpec(tuple(shape[:-1]) + (cols,), lambda i, *_: lead + (i,))


def by_columns(kernel, scalars, arrays, outs, cols, scratch=()):
    steps = arrays[0].shape[-1] // cols
    return pl.pallas_call(
        kernel,
        out_shape=outs,
        grid_spec=pltpu.PrefetchScalarGridSpec(
            num_scalar_prefetch=1,
            grid=(steps,),
            in_specs=[columns(a.shape, cols) for a in arrays],
            out_specs=[columns(o.shape, cols) for o in outs],
            scratch_shapes=scratch,
        ),
        compiler_params=pltpu.CompilerParams(vmem_limit_bytes=40 * 2**20),
    )(scalars, *arrays)


MESH = pl.DeviceIdType.MESH
ANY = pl.BlockSpec(memory_space=pl.ANY)
VMEM = pl.BlockSpec(memory_space=pltpu.VMEM)
SMEM = pl.BlockSpec(memory_space=pltpu.SMEM)


def others(axis, n, body, first=1, last=None):
    me = lax.axis_index(axis)

    def step(d, carry):
        body(lax.rem(me + d, n))
        return carry

    lax.fori_loop(first, n if last is None else last, step, 0)


def meet(axes):
    barrier = pltpu.get_barrier_semaphore()
    for axis, n in axes:
        others(axis, n, lambda p: pl.semaphore_signal(
            barrier, inc=1, device_id={axis: p}, device_id_type=MESH))
    pl.semaphore_wait(barrier, sum(n - 1 for _, n in axes))


def head_exchange(n, xs, out, send, recv, local):
    me = lax.axis_index("head")
    rows, cols = xs[0].shape[0], out.shape[2]

    def copy(i, p):
        return pltpu.make_async_remote_copy(
            src_ref=xs[i].at[:, pl.ds(pl.multiple_of(p * cols, DH), cols)],
            dst_ref=out.at[i, pl.ds(pl.multiple_of(me * rows, rows), rows)],
            send_sem=send.at[i, p],
            recv_sem=recv.at[i, me],
            device_id={"head": p},
            device_id_type=MESH,
        )

    def arrival(i, p):
        return pltpu.make_async_remote_copy(
            src_ref=xs[i].at[:, pl.ds(pl.multiple_of(p * cols, DH), cols)],
            dst_ref=out.at[i, pl.ds(pl.multiple_of(p * rows, rows), rows)],
            send_sem=send.at[i, p],
            recv_sem=recv.at[i, p],
            device_id={"head": p},
            device_id_type=MESH,
        )

    def own(i):
        return pltpu.make_async_copy(
            xs[i].at[:, pl.ds(pl.multiple_of(me * cols, DH), cols)],
            out.at[i, pl.ds(pl.multiple_of(me * rows, rows), rows)],
            local.at[i],
        )

    for i in range(2):
        others("head", n, lambda p: copy(i, p).start())
        own(i).start()

    def wait():
        for i in range(2):
            others("head", n, lambda p: arrival(i, p).wait())
            own(i).wait()

    return wait


def head_sems(n):
    return [
        pltpu.SemaphoreType.DMA((2, n)),
        pltpu.SemaphoreType.DMA((2, n)),
        pltpu.SemaphoreType.DMA((2,)),
    ]


def grid_of(n):
    return (n // 4, 2, 2) if n == 16 else (n // 4, 4, 1)


def gather_kernel(n, hn, k, v, q, g, kv, qg, send, recv, *sems):
    nz, ny, nc = grid_of(n)
    me = lax.axis_index("ctx")
    z, y, c = me // (ny * nc), (me // nc) % ny, me % nc

    def at(z, y, c):
        return (z * ny + y) * nc + c

    def copy(w, shard, peer, way):
        return pltpu.make_async_remote_copy(
            src_ref=kv.at[w, shard],
            dst_ref=kv.at[w, shard],
            send_sem=send.at[w, shard, way],
            recv_sem=recv.at[w, shard],
            device_id={"ctx": peer},
            device_id_type=MESH,
        )

    def across(w, shard):
        return [copy(w, shard, at(z, lax.rem(y + d, ny), c), 1 + d) for d in range(1, ny)]

    def inside(w, shard):
        return [copy(w, shard, at(z, y, lax.rem(c + d, nc)), 1 + ny - 1 + d) for d in range(1, nc)]

    def along(w, shard, up):
        return copy(w, shard, at(z + 1 if up else z - 1, y, c), 0 if up else 1)

    def has_next(up):
        return z + 1 < nz if up else z > 0

    def every_send(do):
        for dist in range(nz):
            for up in (True, False):
                far = z - dist if up else z + dist

                @pl.when((far >= 0) if up else (far < nz))
                def _():
                    for d in range(ny):
                        yy = lax.rem(y + d, ny)
                        shard = at(far, yy, c)
                        if d == 0:
                            do(0, shard, dist, up, True, up or dist > 0)
                        do(1, shard, dist, up, False, up or dist > 0, d)

            for up in (True, False):
                far = z - dist if up else z + dist
                if dist == 0 and not up:
                    continue

                @pl.when((far >= 0) if up else (far < nz))
                def _():
                    for d in range(1, ny):
                        do(0, at(far, lax.rem(y + d, ny), c), dist, None, False, True, d)

    def start(w, shard, dist, up, cross, once, d=0):
        if once and (dist > 0 or d > 0):
            copy(w, shard, at(z, y, c), 0).wait_recv()
        if up is not None:

            @pl.when(has_next(up))
            def _():
                along(w, shard, up).start()

        if once:
            own_line = w == 0 and cross
            own_shard = w == 1 and dist == 0 and d == 0
            for e in (across(w, shard) if own_line or own_shard else []) + inside(w, shard):
                e.start()

    def finish(w, shard, dist, up, cross, once, d=0):
        if up is not None:

            @pl.when(has_next(up))
            def _():
                along(w, shard, up).wait_send()

        if once:
            own_line = w == 0 and cross
            own_shard = w == 1 and dist == 0 and d == 0
            for e in (across(w, shard) if own_line or own_shard else []) + inside(w, shard):
                e.wait_send()

    meet([("ctx", n), ("head", hn)])
    head_exchange(hn, (k, v), kv.at[:, me], *sems[:3])()
    wait_heads = head_exchange(hn, (q, g), qg, *sems[3:])
    every_send(start)
    for d in range(1, nc):
        cc = lax.rem(c + d, nc)

        def arrive(i, carry):
            for w in range(2):
                copy(w, i * nc + cc, at(z, y, c), 0).wait_recv()
            return carry

        lax.fori_loop(0, nz * ny, arrive, 0)
    every_send(finish)
    wait_heads()


def gather(k, v, q, g):
    n, hn = lax.axis_size("ctx"), lax.axis_size("head")
    _, ny, nc = grid_of(n)
    rows, cols = k.shape[0] * hn, k.shape[1] // hn
    return pl.pallas_call(
        functools.partial(gather_kernel, n, hn),
        out_shape=[
            jax.ShapeDtypeStruct((2, n, rows, cols), BF16),
            jax.ShapeDtypeStruct((2, rows, cols), BF16),
        ],
        in_specs=[ANY] * 4,
        out_specs=[ANY] * 2,
        scratch_shapes=[
            pltpu.SemaphoreType.DMA((2, n, ny + nc)),
            pltpu.SemaphoreType.DMA((2, n)),
            *head_sems(hn),
            *head_sems(hn),
        ],
        compiler_params=pltpu.CompilerParams(collective_id=0, has_side_effects=True),
    )(k, v, q, g)


def all_to_all(n, src, dst, send, recv, local):
    me = lax.axis_index("ctx")

    def copy(slot, p):
        return pltpu.make_async_remote_copy(
            src_ref=src(p),
            dst_ref=dst.at[slot],
            send_sem=send.at[p],
            recv_sem=recv.at[slot],
            device_id={"ctx": p},
            device_id_type=MESH,
        )

    own = pltpu.make_async_copy(src(me), dst.at[me], local)

    def start(first=1, last=None):
        others("ctx", n, lambda p: copy(me, p).start(), first, last)
        if first == 1:
            own.start()

    def wait():
        others("ctx", n, lambda p: copy(p, p).wait())
        own.wait()

    return start, wait


def trade_kernel(n, parts, blocks, to_next, to_last, *refs):
    parts_out, blocks_out, from_last, from_next = refs[:4]
    got, piece, s1, r1, s2, r2, s3, r3, s4, r4, local = refs[4:]
    me = lax.axis_index("ctx")
    after, before = lax.rem(me + 1, n), lax.rem(me + n - 1, n)
    meet([("ctx", n)])
    start1, wait1 = all_to_all(n, lambda p: parts.at[p], got, s1, r1, local.at[0])
    start2, wait2 = all_to_all(n, lambda p: piece, parts_out, s2, r2, local.at[1])
    start3, wait3 = all_to_all(n, lambda p: blocks.at[p], blocks_out, s3, r3, local.at[2])
    start1()
    edges = [
        pltpu.make_async_remote_copy(
            src_ref=a,
            dst_ref=b,
            send_sem=s4.at[i],
            recv_sem=r4.at[i],
            device_id={"ctx": p},
            device_id_type=MESH,
        )
        for i, (a, b, p) in enumerate([(to_next, from_last, after), (to_last, from_next, before)])
    ]
    for e in edges:
        e.start()
    start3(1, n // 2)
    wait1()
    total = lax.fori_loop(0, n, lambda i, t: t + got[i].astype(F32), jnp.zeros(piece.shape, F32))
    piece[...] = total.astype(BF16)
    start2()
    start3(n // 2)
    wait2()
    for e in edges:
        e.wait()
    wait3()


def trade(parts, blocks, to_next, to_last):
    n = lax.axis_size("ctx")
    dma = pltpu.SemaphoreType.DMA
    return pl.pallas_call(
        functools.partial(trade_kernel, n),
        out_shape=[jax.ShapeDtypeStruct(a.shape, BF16) for a in (parts, blocks, to_next, to_last)],
        in_specs=[VMEM] + [ANY] * 3,
        out_specs=[ANY] * 4,
        scratch_shapes=[
            pltpu.VMEM(parts.shape, BF16),
            pltpu.VMEM(parts.shape[1:], BF16),
            *[dma((n,))] * 6,
            dma((2,)),
            dma((2,)),
            dma((3,)),
        ],
        compiler_params=pltpu.CompilerParams(collective_id=1, has_side_effects=True),
    )(parts, blocks, to_next, to_last)


def per_device(queries, key_states, value_states, out_grad, random_blocks, global_blocks):
    kv, qg = gather(key_states, value_states, queries, out_grad)
    tokens, cols = kv.shape[2:]
    blocks = tokens // BS
    devices = lax.axis_size("ctx")
    me = lax.axis_index("ctx")
    entries = blocks * NR
    kv = kv.reshape(2, devices * blocks, BS, cols)

    table = random_blocks.reshape(devices, entries)
    served = table // blocks == me
    served_block = jnp.sum(jnp.where(served, table % blocks, 0), axis=1)
    served_used = jnp.any(served, axis=1)
    mine = lax.dynamic_index_in_dim(table, me, 0, keepdims=False)
    global_owner = global_blocks // blocks
    global_offset = global_blocks % blocks
    edge = jnp.stack([jnp.where(me == 0, BS, 0), jnp.where(me == devices - 1, BS, 0)])
    attend_scalars = jnp.concatenate(
        [mine // blocks, edge, mine, (me * blocks)[None], global_blocks]
    ).astype(jnp.int32)
    finish_scalars = jnp.concatenate(
        [
            jnp.where(served_used, served_block, blocks),
            jnp.where(global_owner == me, global_offset, blocks),
        ]
    ).astype(jnp.int32)

    rows = NG * 2 * BS // devices
    width = 2 * DH if cols % (2 * DH) == 0 else DH
    shape = jax.ShapeDtypeStruct
    dq, back, far, own, rim_a, rim_b = by_columns(
        functools.partial(attend_kernel, blocks, width // DH),
        attend_scalars,
        [qg, kv],
        [
            shape((tokens, cols), BF16),
            shape((devices, 2, BS, cols), BF16),
            shape((NG, 2, BS, cols), BF16),
            shape((2, blocks, BS, cols), F32),
            shape((2, BS, cols), BF16),
            shape((2, BS, cols), BF16),
        ],
        width,
    )

    far_sum, arrived, from_last, from_next = trade(
        far.reshape(devices, rows, cols), back, rim_b, rim_a
    )
    far_sum = far_sum.reshape(NG, 2, BS, cols)
    dk, dv = by_columns(
        functools.partial(finish_kernel, blocks, devices),
        finish_scalars,
        [own, arrived, far_sum, from_last, from_next],
        [shape((tokens, cols), BF16)] * 2,
        width,
        [pltpu.VMEM((2, blocks, BS, width), F32)],
    )
    return dq, dk, dv


def solution(mesh):
    placed = P(("ctx", "head"), None)
    return jax.shard_map(
        per_device,
        mesh=mesh,
        in_specs=(placed, placed, placed, placed, P(), P()),
        out_specs=(P("ctx", "head"), P("ctx", "head"), P("ctx", "head")),
        check_vma=False,
    )
```

```python
import functools
import math

import jax
import jax.numpy as jnp
from jax import lax
from jax.experimental import pallas as pl
from jax.experimental.pallas import tpu as pltpu
from jax.sharding import PartitionSpec as P

DH = 128
BS = 32
NR = 3
NG = 4
F32 = jnp.float32
BF16 = jnp.bfloat16


def dot(a, b, dims):
    return lax.dot_general(a, b, (dims, ((), ())), preferred_element_type=F32)


def attend_kernel(
    blocks, heads, sc, qg, kv, dq, back, far, own, rim_a, rim_b
):
    inv_root = 1.0 / math.sqrt(DH)
    entries = blocks * NR
    for h in range(heads):
        c = slice(h * DH, (h + 1) * DH)
        back[:, :, :, c] = jnp.zeros((back.shape[0], 2, BS, DH), BF16)
        gk, gv = ([kv[w, sc[2 * entries + 3 + i], :, c] for i in range(NG)] for w in range(2))
        first, final = sc[2 * entries + 2], kv.shape[1] - 1
        totals = [[None] * blocks, [None] * blocks]
        far_total = [None, None]
        staged, ready = [], []

        def add(which, m, part):
            old = totals[which][m]
            totals[which][m] = part if old is None else old + part

        for n in range(blocks):
            rows = slice(n * BS, (n + 1) * BS)
            qn, gn = qg[0, rows, c], qg[1, rows, c]

            def listed(w, far_list):
                at = [jnp.maximum(first + n - 1, 0), first + n, jnp.minimum(first + n + 1, final)]
                at += [sc[entries + 2 + n * NR + j] for j in range(NR)]
                out = [kv[w, m, :, c] for m in at]
                return jnp.concatenate(out + far_list, axis=0)

            kn, vn = listed(0, gk), listed(1, gv)
            s = dot(qn, kn, ((1,), (1,))) * inv_root
            dp = dot(gn, vn, ((1,), (1,)))
            if n == 0 or n == blocks - 1:
                col = lax.broadcasted_iota(jnp.int32, s.shape, 1)
                if n == 0:
                    s = jnp.where(col < sc[entries], -jnp.inf, s)
                if n == blocks - 1:
                    bad = (col >= 2 * BS) & (col < 2 * BS + sc[entries + 1])
                    s = jnp.where(bad, -jnp.inf, s)
            staged.append((rows, qn, gn, kn, s, dp))

        for n, (rows, qn, gn, kn, s, dp) in enumerate(staged):
            e = jnp.exp(s - jnp.max(s, axis=1, keepdims=True))
            p = e / jnp.sum(e, axis=1, keepdims=True)
            ph = p.astype(BF16)
            row_dot = jnp.sum(ph.astype(F32) * dp, axis=1, keepdims=True)
            ds = (p * (dp - row_dot)).astype(BF16)
            ready.append((rows, qn, gn, kn, ph, ds))

        for n, (rows, qn, gn, kn, ph, ds) in enumerate(ready):
            dq[rows, c] = (dot(ds, kn, ((1,), (0,))) * inv_root).astype(BF16)
            for w, part in (
                (0, dot(ds, qn, ((0,), (0,))) * inv_root),
                (1, dot(ph, gn, ((0,), (0,)))),
            ):
                if n == 0:
                    rim_a[w, :, c] = part[:BS].astype(BF16)
                else:
                    add(w, n - 1, part[:BS])
                add(w, n, part[BS : 2 * BS])
                if n == blocks - 1:
                    rim_b[w, :, c] = part[2 * BS : 3 * BS].astype(BF16)
                else:
                    add(w, n + 1, part[2 * BS : 3 * BS])
                for j in range(NR):
                    piece = part[(3 + j) * BS : (4 + j) * BS].astype(BF16)
                    back[sc[n * NR + j], w, :, c] = piece
                tail = part[(3 + NR) * BS :]
                far_total[w] = tail if far_total[w] is None else far_total[w] + tail
        for w in range(2):
            for m in range(blocks):
                own[w, m, :, c] = totals[w][m]
            for i in range(NG):
                far[i, w, :, c] = far_total[w][i * BS : (i + 1) * BS].astype(BF16)


def finish_kernel(blocks, devices, sc, own, arrived, far, rim_a, rim_b, dk, dv, acc):
    acc[...] = own[...]
    acc[:, 0] += rim_a[...].astype(F32)
    acc[:, blocks - 1] += rim_b[...].astype(F32)
    for r in range(devices):
        @pl.when(sc[r] < blocks)
        def _():
            acc[:, sc[r]] += arrived[r].astype(F32)
    for g in range(NG):
        @pl.when(sc[devices + g] < blocks)
        def _():
            acc[:, sc[devices + g]] += far[g].astype(F32)
    for w, out in ((0, dk), (1, dv)):
        for m in range(blocks):
            out[m * BS : (m + 1) * BS, :] = acc[w, m].astype(BF16)


def columns(shape, cols):
    lead = (0,) * (len(shape) - 1)
    return pl.BlockSpec(tuple(shape[:-1]) + (cols,), lambda i, *_: lead + (i,))


def by_columns(kernel, scalars, arrays, outs, cols, scratch=()):
    steps = arrays[0].shape[-1] // cols
    return pl.pallas_call(
        kernel,
        out_shape=outs,
        grid_spec=pltpu.PrefetchScalarGridSpec(
            num_scalar_prefetch=1,
            grid=(steps,),
            in_specs=[columns(a.shape, cols) for a in arrays],
            out_specs=[columns(o.shape, cols) for o in outs],
            scratch_shapes=scratch,
        ),
        compiler_params=pltpu.CompilerParams(vmem_limit_bytes=40 * 2**20),
    )(scalars, *arrays)


MESH = pl.DeviceIdType.MESH
ANY = pl.BlockSpec(memory_space=pl.ANY)
VMEM = pl.BlockSpec(memory_space=pltpu.VMEM)
SMEM = pl.BlockSpec(memory_space=pltpu.SMEM)


def others(axis, n, body, first=1, last=None):
    me = lax.axis_index(axis)

    def step(d, carry):
        body(lax.rem(me + d, n))
        return carry

    lax.fori_loop(first, n if last is None else last, step, 0)


def meet(axes):
    barrier = pltpu.get_barrier_semaphore()
    for axis, n in axes:
        others(axis, n, lambda p: pl.semaphore_signal(
            barrier, inc=1, device_id={axis: p}, device_id_type=MESH))
    pl.semaphore_wait(barrier, sum(n - 1 for _, n in axes))


def head_exchange(n, xs, out, send, recv, local):
    me = lax.axis_index("head")
    rows, cols = xs[0].shape[0], out.shape[2]

    def copy(i, p):
        return pltpu.make_async_remote_copy(
            src_ref=xs[i].at[:, pl.ds(pl.multiple_of(p * cols, DH), cols)],
            dst_ref=out.at[i, pl.ds(pl.multiple_of(me * rows, rows), rows)],
            send_sem=send.at[i, p],
            recv_sem=recv.at[i, me],
            device_id={"head": p},
            device_id_type=MESH,
        )

    def arrival(i, p):
        return pltpu.make_async_remote_copy(
            src_ref=xs[i].at[:, pl.ds(pl.multiple_of(p * cols, DH), cols)],
            dst_ref=out.at[i, pl.ds(pl.multiple_of(p * rows, rows), rows)],
            send_sem=send.at[i, p],
            recv_sem=recv.at[i, p],
            device_id={"head": p},
            device_id_type=MESH,
        )

    def own(i):
        return pltpu.make_async_copy(
            xs[i].at[:, pl.ds(pl.multiple_of(me * cols, DH), cols)],
            out.at[i, pl.ds(pl.multiple_of(me * rows, rows), rows)],
            local.at[i],
        )

    for i in range(2):
        others("head", n, lambda p: copy(i, p).start())
        own(i).start()

    def wait():
        for i in range(2):
            others("head", n, lambda p: arrival(i, p).wait())
            own(i).wait()

    return wait


def head_sems(n):
    return [
        pltpu.SemaphoreType.DMA((2, n)),
        pltpu.SemaphoreType.DMA((2, n)),
        pltpu.SemaphoreType.DMA((2,)),
    ]


def grid_of(n):
    return (n // 4, 2, 2) if n == 16 else (n // 4, 4, 1)


def gather_kernel(n, hn, k, v, q, g, kv, qg, send, recv, *sems):
    nz, ny, nc = grid_of(n)
    me = lax.axis_index("ctx")
    z, y, c = me // (ny * nc), (me // nc) % ny, me % nc

    def at(z, y, c):
        return (z * ny + y) * nc + c

    def copy(w, shard, peer, way):
        return pltpu.make_async_remote_copy(
            src_ref=kv.at[w, shard],
            dst_ref=kv.at[w, shard],
            send_sem=send.at[w, shard, way],
            recv_sem=recv.at[w, shard],
            device_id={"ctx": peer},
            device_id_type=MESH,
        )

    def across(w, shard):
        return [copy(w, shard, at(z, lax.rem(y + d, ny), c), 1 + d) for d in range(1, ny)]

    def inside(w, shard):
        return [copy(w, shard, at(z, y, lax.rem(c + d, nc)), 1 + ny - 1 + d) for d in range(1, nc)]

    def along(w, shard, up):
        return copy(w, shard, at(z + 1 if up else z - 1, y, c), 0 if up else 1)

    def has_next(up):
        return z + 1 < nz if up else z > 0

    def every_send(do):
        for dist in range(nz):
            for up in (True, False):
                far = z - dist if up else z + dist

                @pl.when((far >= 0) if up else (far < nz))
                def _():
                    for d in range(ny):
                        yy = lax.rem(y + d, ny)
                        shard = at(far, yy, c)
                        if d == 0:
                            do(0, shard, dist, up, True, up or dist > 0)
                        do(1, shard, dist, up, False, up or dist > 0, d)

            for up in (True, False):
                far = z - dist if up else z + dist
                if dist == 0 and not up:
                    continue

                @pl.when((far >= 0) if up else (far < nz))
                def _():
                    for d in range(1, ny):
                        do(0, at(far, lax.rem(y + d, ny), c), dist, None, False, True, d)

    def start(w, shard, dist, up, cross, once, d=0):
        if once and (dist > 0 or d > 0):
            copy(w, shard, at(z, y, c), 0).wait_recv()
        if up is not None:

            @pl.when(has_next(up))
            def _():
                along(w, shard, up).start()

        if once:
            own_line = w == 0 and cross
            own_shard = w == 1 and dist == 0 and d == 0
            for e in (across(w, shard) if own_line or own_shard else []) + inside(w, shard):
                e.start()

    def finish(w, shard, dist, up, cross, once, d=0):
        if up is not None:

            @pl.when(has_next(up))
            def _():
                along(w, shard, up).wait_send()

        if once:
            own_line = w == 0 and cross
            own_shard = w == 1 and dist == 0 and d == 0
            for e in (across(w, shard) if own_line or own_shard else []) + inside(w, shard):
                e.wait_send()

    meet([("ctx", n), ("head", hn)])
    head_exchange(hn, (k, v), kv.at[:, me], *sems[:3])()
    wait_heads = head_exchange(hn, (q, g), qg, *sems[3:])
    every_send(start)
    for d in range(1, nc):
        cc = lax.rem(c + d, nc)

        def arrive(i, carry):
            for w in range(2):
                copy(w, i * nc + cc, at(z, y, c), 0).wait_recv()
            return carry

        lax.fori_loop(0, nz * ny, arrive, 0)
    every_send(finish)
    wait_heads()


def gather(k, v, q, g):
    n, hn = lax.axis_size("ctx"), lax.axis_size("head")
    _, ny, nc = grid_of(n)
    rows, cols = k.shape[0] * hn, k.shape[1] // hn
    return pl.pallas_call(
        functools.partial(gather_kernel, n, hn),
        out_shape=[
            jax.ShapeDtypeStruct((2, n, rows, cols), BF16),
            jax.ShapeDtypeStruct((2, rows, cols), BF16),
        ],
        in_specs=[ANY] * 4,
        out_specs=[ANY] * 2,
        scratch_shapes=[
            pltpu.SemaphoreType.DMA((2, n, ny + nc)),
            pltpu.SemaphoreType.DMA((2, n)),
            *head_sems(hn),
            *head_sems(hn),
        ],
        compiler_params=pltpu.CompilerParams(collective_id=0, has_side_effects=True),
    )(k, v, q, g)


def all_to_all(n, src, dst, send, recv, local):
    me = lax.axis_index("ctx")

    def copy(slot, p):
        return pltpu.make_async_remote_copy(
            src_ref=src(p),
            dst_ref=dst.at[slot],
            send_sem=send.at[p],
            recv_sem=recv.at[slot],
            device_id={"ctx": p},
            device_id_type=MESH,
        )

    own = pltpu.make_async_copy(src(me), dst.at[me], local)

    def start(first=1, last=None):
        others("ctx", n, lambda p: copy(me, p).start(), first, last)
        if first == 1:
            own.start()

    def wait():
        others("ctx", n, lambda p: copy(p, p).wait())
        own.wait()

    return start, wait


def trade_kernel(n, parts, blocks, to_next, to_last, *refs):
    parts_out, blocks_out, from_last, from_next = refs[:4]
    got, piece, s1, r1, s2, r2, s3, r3, s4, r4, local = refs[4:]
    me = lax.axis_index("ctx")
    after, before = lax.rem(me + 1, n), lax.rem(me + n - 1, n)
    meet([("ctx", n)])
    start1, wait1 = all_to_all(n, lambda p: parts.at[p], got, s1, r1, local.at[0])
    start2, wait2 = all_to_all(n, lambda p: piece, parts_out, s2, r2, local.at[1])
    start3, wait3 = all_to_all(n, lambda p: blocks.at[p], blocks_out, s3, r3, local.at[2])
    start1()
    edges = [
        pltpu.make_async_remote_copy(
            src_ref=a,
            dst_ref=b,
            send_sem=s4.at[i],
            recv_sem=r4.at[i],
            device_id={"ctx": p},
            device_id_type=MESH,
        )
        for i, (a, b, p) in enumerate([(to_next, from_last, after), (to_last, from_next, before)])
    ]
    for e in edges:
        e.start()
    start3(n // 4, n - n // 4)
    wait1()
    total = lax.fori_loop(0, n, lambda i, t: t + got[i].astype(F32), jnp.zeros(piece.shape, F32))
    piece[...] = total.astype(BF16)
    start2()
    start3(1, n // 4)
    start3(n - n // 4)
    wait2()
    for e in edges:
        e.wait()
    wait3()


def trade(parts, blocks, to_next, to_last):
    n = lax.axis_size("ctx")
    dma = pltpu.SemaphoreType.DMA
    return pl.pallas_call(
        functools.partial(trade_kernel, n),
        out_shape=[jax.ShapeDtypeStruct(a.shape, BF16) for a in (parts, blocks, to_next, to_last)],
        in_specs=[VMEM] + [ANY] * 3,
        out_specs=[ANY] * 4,
        scratch_shapes=[
            pltpu.VMEM(parts.shape, BF16),
            pltpu.VMEM(parts.shape[1:], BF16),
            *[dma((n,))] * 6,
            dma((2,)),
            dma((2,)),
            dma((3,)),
        ],
        compiler_params=pltpu.CompilerParams(collective_id=1, has_side_effects=True),
    )(parts, blocks, to_next, to_last)


def per_device(queries, key_states, value_states, out_grad, random_blocks, global_blocks):
    kv, qg = gather(key_states, value_states, queries, out_grad)
    tokens, cols = kv.shape[2:]
    blocks = tokens // BS
    devices = lax.axis_size("ctx")
    me = lax.axis_index("ctx")
    entries = blocks * NR
    kv = kv.reshape(2, devices * blocks, BS, cols)

    table = random_blocks.reshape(devices, entries)
    served = table // blocks == me
    served_block = jnp.sum(jnp.where(served, table % blocks, 0), axis=1)
    served_used = jnp.any(served, axis=1)
    mine = lax.dynamic_index_in_dim(table, me, 0, keepdims=False)
    global_owner = global_blocks // blocks
    global_offset = global_blocks % blocks
    edge = jnp.stack([jnp.where(me == 0, BS, 0), jnp.where(me == devices - 1, BS, 0)])
    attend_scalars = jnp.concatenate(
        [mine // blocks, edge, mine, (me * blocks)[None], global_blocks]
    ).astype(jnp.int32)
    finish_scalars = jnp.concatenate(
        [
            jnp.where(served_used, served_block, blocks),
            jnp.where(global_owner == me, global_offset, blocks),
        ]
    ).astype(jnp.int32)

    rows = NG * 2 * BS // devices
    width = 2 * DH if cols % (2 * DH) == 0 else DH
    shape = jax.ShapeDtypeStruct
    dq, back, far, own, rim_a, rim_b = by_columns(
        functools.partial(attend_kernel, blocks, width // DH),
        attend_scalars,
        [qg, kv],
        [
            shape((tokens, cols), BF16),
            shape((devices, 2, BS, cols), BF16),
            shape((NG, 2, BS, cols), BF16),
            shape((2, blocks, BS, cols), F32),
            shape((2, BS, cols), BF16),
            shape((2, BS, cols), BF16),
        ],
        width,
    )

    far_sum, arrived, from_last, from_next = trade(
        far.reshape(devices, rows, cols), back, rim_b, rim_a
    )
    far_sum = far_sum.reshape(NG, 2, BS, cols)
    dk, dv = by_columns(
        functools.partial(finish_kernel, blocks, devices),
        finish_scalars,
        [own, arrived, far_sum, from_last, from_next],
        [shape((tokens, cols), BF16)] * 2,
        width,
        [pltpu.VMEM((2, blocks, BS, width), F32)],
    )
    return dq, dk, dv


def solution(mesh):
    placed = P(("ctx", "head"), None)
    return jax.shard_map(
        per_device,
        mesh=mesh,
        in_specs=(placed, placed, placed, placed, P(), P()),
        out_specs=(P("ctx", "head"), P("ctx", "head"), P("ctx", "head")),
        check_vma=False,
    )
```
